128 devices in a mesh: row: 16 (over y, x_lo, core), col: 8 (over z, x_hi).
Axes of the slice: x: 4 (x_hi: 2, x_lo: 2; x = x_hi * 2 + x_lo), y: 4, z: 4, core: 2. Of those that a mesh axis runs over, the one named last changes fastest.
Arguments:
- grad_flat: bfloat16 [8192, 4096], P(('row', 'col')), may hold values from -6 to 6
- out_factor_inv: bfloat16 [8192, 8192], P('row', 'col'), may hold values from -0.05 to 2.05
- in_factor_inv: bfloat16 [4096, 16384], P(('row', 'col')), may hold values from -0.05 to 2.05
Outputs:
- preconditioned: float32 [8192, 16384], P('row', 'col')
The draws below stay inside these ranges and needn't reach their ends.
All inputs are finite; a program needn't handle non-finite values.
Results may differ from the reference program's by a relative error of at most 0.003.
Values may be sent and summed in bfloat16 or wider, within the bound.
A program may use at most 128 MiB of HBM per device.

```python
import math
import jax
import jax.numpy as jnp
from jax import lax

M = 8192
KP = 4096
N = 16384


def draw_out_factor_inv(key, part):
    key = jax.random.fold_in(key, 11)
    key_off, key_diag = jax.random.split(key)
    spread = jax.random.truncated_normal(key_off, -6.0, 6.0, (M, M), jnp.float32) * (0.5 / math.sqrt(M))
    scales = jnp.exp(jax.random.uniform(key_diag, (M,), jnp.float32, math.log(0.5), math.log(2.0)))
    row_ids = lax.broadcasted_iota(jnp.int32, (M, M), 0)
    col_ids = lax.broadcasted_iota(jnp.int32, (M, M), 1)
    return (spread + jnp.where(row_ids == col_ids, scales[None, :], 0.0)).astype(jnp.bfloat16)


def draw_in_factor_inv(key, part):
    key = jax.random.fold_in(key, 23)
    key_off, key_diag = jax.random.split(key)
    spread = jax.random.truncated_normal(key_off, -6.0, 6.0, (KP, N), jnp.float32) * (0.5 / math.sqrt(KP))
    scales = jnp.exp(jax.random.uniform(key_diag, (N,), jnp.float32, math.log(0.5), math.log(2.0)))
    row_ids = lax.broadcasted_iota(jnp.int32, (KP, N), 0)
    col_ids = lax.broadcasted_iota(jnp.int32, (KP, N), 1)
    return (spread + jnp.where(row_ids == col_ids, scales[None, :], 0.0)).astype(jnp.bfloat16)


def block_scale(rng, shape, cuts, least, top_value):
    factor_of, own = 1.0, jax.random.fold_in(rng, 6)
    for position, shards_of in cuts:
        heights = jnp.exp(jax.random.uniform(jax.random.fold_in(own, position), (shards_of,), jnp.float32, least / len(cuts), top_value / len(cuts)))
        factor_of = factor_of * jnp.repeat(heights, shape[position] // shards_of).reshape([-1 if axis == position else 1 for axis in range(len(shape))])
    return factor_of


def normal_values(rng, shape, scale, bound, cuts=(), kind=jnp.bfloat16):
    loudness = block_scale(rng, shape, cuts, -0.22, 0.18) if cuts else 1.0
    values = jax.random.normal(rng, shape, jnp.float32) * scale * loudness
    return jnp.minimum(jnp.maximum(values, -bound), bound).astype(kind)


def setup_inputs(seed: int = 0) -> dict:
    seeds = jax.random.split(jax.random.key(seed), 4)
    grad_flat = normal_values(seeds[0], (M, KP), 1.0, 6.0, ((0, 128),))
    out_factor_inv = draw_out_factor_inv(jax.random.fold_in(seeds[3], 71), 0)
    in_factor_inv = draw_in_factor_inv(jax.random.fold_in(seeds[3], 71), 0)
    return dict(grad_flat=grad_flat, out_factor_inv=out_factor_inv, in_factor_inv=in_factor_inv)


def reference(grad_flat, out_factor_inv, in_factor_inv):
    left = jnp.dot(out_factor_inv, grad_flat, preferred_element_type=jnp.float32).astype(jnp.bfloat16)
    return jnp.dot(left, in_factor_inv, preferred_element_type=jnp.float32)
```

```python
import functools

import jax
import jax.numpy as jnp
from jax import lax
from jax.experimental import pallas as pl
from jax.experimental.pallas import tpu as pltpu
from jax.sharding import PartitionSpec as P

MESH = pl.DeviceIdType.MESH

PARTS = {"A": 2, "L": 2, "G": 2, "F": 4}
UNITS = {"A": 1.0, "L": 0.5, "G": 0.5, "F": 0.5}
RELIEF = {"A": True, "L": True, "G": False, "F": False}
OWN = -1


def plan(array, slot, part):
    ahead, behind = ("+", "-") if part % 2 == 0 else ("-", "+")
    sends = {
        OWN: [("x", 0), (ahead, 1), (behind, 2)],
        0: [(ahead, 3)] + ([] if RELIEF[array] else [(behind, 4)]),
        1: [(ahead, 5)],
        2: [("x", 4)] if RELIEF[array] else [],
        4: [(behind, 6)],
    }.get(slot, [])
    if array in "GF" and slot < 7:
        sends = sends + [("core", 8 + slot)]
    return sends


def relative(slot, part):
    sibling, slot = (1, slot - 8) if slot >= 7 else (0, slot)
    step, other = {OWN: (0, 0), 0: (0, 1), 1: (3, 0), 2: (1, 0), 3: (3, 1), 4: (1, 1), 5: (2, 0), 6: (2, 1)}[slot]
    return (step if part % 2 == 0 else (4 - step) % 4), other, sibling


def schedule():
    free, pending, order = {}, [], []
    unit = 11.3

    def send(now, array, slot, part):
        for link, there in plan(array, slot, part):
            key = link if link in ("x", "core") else link + ("z" if array in "AL" else "y")
            took = UNITS[array] * (unit if link != "core" else 1.8)
            start = max(now, free.get(key, 0.0))
            free[key] = start + took
            pending.append((start + took + 1.0, array, there, part))

    for key in ("x", "+z", "-z"):
        free[key] = 17.0
    pending += [(1.0, "A", OWN, p) for p in range(PARTS["A"])]
    pending += [(8.0, "G", OWN, p) for p in range(PARTS["G"])]
    pending += [(24.0, "F", OWN, p) for p in range(PARTS["F"])]
    seen = {}
    while pending:
        pending.sort()
        event = pending.pop(0)
        now, array, slot, part = event
        order.append(event)
        send(now, array, slot, part)
        seen.setdefault((array, part), []).append(now)
        if array == "G" and sum(len(seen.get(("G", p), [])) for p in range(PARTS["G"])) == 16 * PARTS["G"]:
            seen["G"] = now
        if array in "AG" and "G" in seen:
            for p in range(PARTS["A"]):
                if len(seen.get(("A", p), [])) == 8 and ("L", p) not in seen:
                    seen[("L", p)] = []
                    pending.append((now + 1.5, "L", OWN, p))
    return order


def pick(index, values):
    chosen = values[0]
    for position, value in enumerate(values[1:], 1):
        chosen = jnp.where(index == position, value, chosen)
    return chosen


def kernel(order, grad, outer, inner, result, a_buf, g_buf, f_buf, l_buf, l_sum, c_sum, *sems):
    send_sem = dict(zip("AGFL", sems[0:4]))
    recv_sem = dict(zip("AGFL", sems[4:8]))
    swap_send, swap_recv, local_sem, out_sem = sems[8:]
    row, col = lax.axis_index("row"), lax.axis_index("col")
    y, x_lo, core = row // 4, (row // 2) % 2, row % 2
    z, x_hi = col // 2, col % 2

    def row_of(step, other, sibling=0):
        return ((y + step) % 4) * 4 + (x_lo + other) % 2 * 2 + (core + sibling) % 2

    def col_of(step, other):
        return ((z + step) % 4) * 2 + (x_hi + other) % 2

    def device(array, link):
        if link == "core":
            return (row_of(0, 0, 1), col)
        step, other = {"x": (0, 1), "+": (1, 0), "-": (3, 0)}[link]
        return (row, col_of(step, other)) if array in "AL" else (row_of(step, other), col)

    def block_id(array, slot, part):
        step, other, sibling = relative(slot, part)
        return col_of(step, other) if array in "AL" else row_of(step, other, sibling)

    buffers = {"A": a_buf, "G": g_buf, "F": f_buf, "L": l_buf}

    def view(array, block, part):
        buffer = buffers[array]
        if array == "F":
            width = buffer.shape[2] // PARTS["F"]
            return buffer.at[block, :, pl.ds(part * width, width)]
        height = buffer.shape[1] // PARTS[array]
        return buffer.at[block, pl.ds(part * height, height), :]

    def copy(array, slot, part, link, there):
        here = view(array, block_id(array, slot, part), part)
        return pltpu.make_async_remote_copy(
            src_ref=here,
            dst_ref=here,
            send_sem=send_sem[array].at[there, part],
            recv_sem=recv_sem[array].at[there, part],
            device_id=device(array, link),
            device_id_type=MESH,
        )

    def wait_recv(array, slot, part):
        here = view(array, block_id(array, slot, part), part)
        pltpu.make_async_remote_copy(
            src_ref=here,
            dst_ref=here,
            send_sem=send_sem[array].at[slot, part],
            recv_sem=recv_sem[array].at[slot, part],
            device_id=device(array, "x"),
            device_id_type=MESH,
        ).wait_recv()

    sent = []

    def forward(array, slot, part):
        for link, there in plan(array, slot, part):
            outgoing = copy(array, slot, part, link, there)
            outgoing.start()
            sent.append(outgoing)

    locals_ = [
        pltpu.make_async_copy(outer, a_buf.at[col], local_sem.at[0]),
        pltpu.make_async_copy(
            grad.at[:, pl.ds(pl.multiple_of(col * 512, 512), 512)],
            g_buf.at[row, pl.ds(pl.multiple_of(col * 64, 64), 64), :],
            local_sem.at[1],
        ),
        pltpu.make_async_copy(
            inner.at[:, pl.ds(pl.multiple_of(col * 2048, 2048), 2048)],
            f_buf.at[row, pl.ds(pl.multiple_of(col * 32, 32), 32), :],
            local_sem.at[2],
        ),
    ]
    for one in locals_:
        one.start()

    barrier = pltpu.get_barrier_semaphore()
    peers = [(row, lax.rem(col + k, 8)) for k in range(1, 8)]
    peers += [device("G", link) for link in ("x", "+", "-", "core")]
    for peer in peers:
        pl.semaphore_signal(barrier, inc=1, device_id=peer, device_id_type=MESH)
    pl.semaphore_wait(barrier, len(peers))

    def swap(which, k):
        source, buffer, height, width = ((grad, g_buf, 64, 512), (inner, f_buf, 32, 2048))[which]
        to = lax.rem(col + k, 8)
        return pltpu.make_async_remote_copy(
            src_ref=source.at[:, pl.ds(pl.multiple_of(to * width, width), width)],
            dst_ref=buffer.at[row, pl.ds(pl.multiple_of(col * height, height), height), :],
            send_sem=swap_send.at[which, k],
            recv_sem=swap_recv.at[which, k],
            device_id=(row, to),
            device_id_type=MESH,
        )

    def swap_wait(which, k):
        source, buffer, height, width = ((grad, g_buf, 64, 512), (inner, f_buf, 32, 2048))[which]
        sender = lax.rem(col + 8 - k, 8)
        pltpu.make_async_remote_copy(
            src_ref=source.at[:, pl.ds(0, width)],
            dst_ref=buffer.at[row, pl.ds(pl.multiple_of(sender * height, height), height), :],
            send_sem=swap_send.at[which, k],
            recv_sem=swap_recv.at[which, k],
            device_id=(row, sender),
            device_id_type=MESH,
        ).wait_recv()

    def start_swap(which):
        for k in (4, 3, 5, 2, 6, 1, 7):
            outgoing = swap(which, k)
            outgoing.start()
            sent.append(outgoing)

    start_swap(0)

    def add_left(block, part):
        rows = pl.ds(part * 256 if isinstance(part, int) else pl.multiple_of(part * 256, 256), 256)
        grads = g_buf[pl.ds(block * 2, 2)].reshape(1024, 512)
        l_sum[rows, :] += jnp.dot(a_buf[block, rows, :], grads, preferred_element_type=jnp.float32)

    def add_result(block, part):
        columns = pl.ds(part * 512 if isinstance(part, int) else pl.multiple_of(part * 512, 512), 512)
        weights = f_buf[pl.ds(block * 2, 2), :, columns].reshape(512, 512)
        c_sum[:, columns] += jnp.dot(l_buf[block], weights, preferred_element_type=jnp.float32)

    def each(pairs, act):
        if len(pairs) < 2:
            for pair in pairs:
                act(*pair)
            return

        @pl.loop(0, len(pairs))
        def _(k):
            act(pick(k, [p[0] for p in pairs]), pick(k, [p[1] for p in pairs]))

    counts = dict.fromkeys("AGFL", 0)
    counts.update({("F", p): 0 for p in range(PARTS["F"])})
    pending_left, ready_l, ready_f, out_copies = [], [], [], []
    blocks_l = {}
    done = [0] * PARTS["F"]

    def multiply(pairs):
        last = any(done[p] == 7 for _, p in pairs)
        for group in [[pair] for pair in pairs] if last else [pairs]:
            each(group, add_result)
            for _, p in group:
                done[p] += 1
                if done[p] == 8:
                    columns = pl.ds(p * 512, 512)
                    out = pltpu.make_async_copy(c_sum.at[:, columns], result.at[:, columns], out_sem.at[p])
                    out.start()
                    out_copies.append(out)

    for _, array, slot, part in order:
        if slot == OWN:
            if array == "A":
                if part == 0:
                    locals_[0].wait()
                forward("A", OWN, part)
                if part == PARTS["A"] - 1:
                    start_swap(1)
                    l_sum[...] = jnp.zeros_like(l_sum)

                    @pl.loop(0, 8)
                    def _(k):
                        rows = pl.ds(pl.multiple_of(k * 64, 64), 64)
                        c_sum[rows, :] = jnp.zeros((64, 2048), jnp.float32)
            elif array == "L":
                l_buf[col, pl.ds(part * 256, 256), :] = l_sum[pl.ds(part * 256, 256), :].astype(jnp.bfloat16)
                forward("L", OWN, part)
            else:
                which = "GF".index(array)
                if part == 0:
                    locals_[1 + which].wait()
                    for k in range(1, 8):
                        swap_wait(which, k)
                forward(array, OWN, part)
        else:
            wait_recv(array, slot, part)
            if slot < 7:
                forward(array, slot, part)
        counts[array] += 1
        if array == "A":
            pending_left.append((block_id("A", slot, part), part))
        if array in "AG" and counts["G"] == 16 * PARTS["G"]:
            each(pending_left, add_left)
            pending_left.clear()
        if array == "L":
            place = relative(slot, part)
            blocks_l[place] = blocks_l.get(place, 0) + 1
            if blocks_l[place] == PARTS["L"]:
                ready_l.append(block_id("L", slot, part))
                multiply([(ready_l[-1], p) for p in ready_f])
        if array == "F":
            counts[("F", part)] += 1
            if counts[("F", part)] == 16:
                ready_f.append(part)
                multiply([(block, part) for block in ready_l])

    for one in sent:
        one.wait_send()
    for out in out_copies:
        out.wait()


def per_device(grad_flat, out_factor_inv, in_factor_inv):
    order = schedule()
    dma = pltpu.SemaphoreType.DMA
    return pl.pallas_call(
        functools.partial(kernel, order),
        out_shape=jax.ShapeDtypeStruct((512, 2048), jnp.float32),
        in_specs=[pl.BlockSpec(memory_space=pl.ANY)] * 3,
        out_specs=pl.BlockSpec(memory_space=pl.ANY),
        scratch_shapes=[
            pltpu.VMEM((8, 512, 1024), jnp.bfloat16),
            pltpu.VMEM((16, 512, 512), jnp.bfloat16),
            pltpu.VMEM((16, 256, 2048), jnp.bfloat16),
            pltpu.VMEM((8, 512, 512), jnp.bfloat16),
            pltpu.VMEM((512, 512), jnp.float32),
            pltpu.VMEM((512, 2048), jnp.float32),
            dma((7, PARTS["A"])),
            dma((15, PARTS["G"])),
            dma((15, PARTS["F"])),
            dma((7, PARTS["L"])),
            dma((7, PARTS["A"])),
            dma((15, PARTS["G"])),
            dma((15, PARTS["F"])),
            dma((7, PARTS["L"])),
            dma((2, 8)),
            dma((2, 8)),
            dma((3,)),
            dma((PARTS["F"],)),
        ],
        compiler_params=pltpu.CompilerParams(
            collective_id=0, has_side_effects=True, vmem_limit_bytes=60 * 2**20
        ),
    )(grad_flat, out_factor_inv, in_factor_inv)


def solution(mesh):
    return jax.shard_map(
        per_device,
        mesh=mesh,
        in_specs=(P(("row", "col"), None), P("row", "col"), P(("row", "col"), None)),
        out_specs=P("row", "col"),
        check_vma=False,
    )
```

```python
import functools

import jax
import jax.numpy as jnp
from jax import lax
from jax.experimental import pallas as pl
from jax.experimental.pallas import tpu as pltpu
from jax.sharding import PartitionSpec as P

MESH = pl.DeviceIdType.MESH

PARTS = {"A": 2, "L": 2, "G": 2, "F": 4}
UNITS = {"A": 1.0, "L": 0.5, "G": 0.5, "F": 0.5}
RELIEF = {"A": False, "L": True, "G": False, "F": False}
OWN, OWN_X, START = -1, -2, -3
RELAYED = 4
UNIT, LAG, FIFO = 12.0, 1.5, True


def plan(array, slot, part):
    ahead, behind = ("+", "-") if part % 2 == 0 else ("-", "+")
    sends = {
        OWN: [(ahead, 1), (behind, 2)],
        OWN_X: [("x", 0)],
        0: [(ahead, 3)] + ([] if RELIEF[array] else [(behind, 4)]),
        1: [(ahead, 5)],
        2: [("x", 4)] if RELIEF[array] else [],
        4: [(behind, 6)],
    }.get(slot, [])
    if array in "GF" and OWN <= slot < 7:
        sends = sends + [("core", 8 + slot)]
    return sends


def relative(slot, part):
    sibling, slot = (1, slot - 8) if slot >= 7 else (0, slot)
    step, other = {OWN: (0, 0), OWN_X: (0, 0), 0: (0, 1), 1: (3, 0), 2: (1, 0), 3: (3, 1), 4: (1, 1), 5: (2, 0), 6: (2, 1)}[slot]
    return (step if part % 2 == 0 else (4 - step) % 4), other, sibling


def schedule():
    now, active, timers, order, seen = 0.0, [], [], [], {}
    swaps, starts, relayed = {("G", 0): 3, ("F", 0): 3}, {}, 0

    def send(array, slot, part):
        for link, there in plan(array, slot, part):
            key = link if link in ("x", "core") else link + ("z" if array in "AL" else "y")
            active.append([UNITS[array] * (UNIT if link != "core" else 1.8), key, (array, there, part)])

    for key in ("x", "+z", "-z"):
        active.append([0.5 * UNIT, key, ("swap", "G", 0)])
    timers += [(0.5, ("A", OWN, 0))]
    while active or timers:
        on = {}
        for entry in active:
            on.setdefault(entry[1], []).append(entry)
        if FIFO:
            on = {key: entries[:1] for key, entries in on.items()}
        ends = [entry[0] * len(entries) for entries in on.values() for entry in entries]
        step = min(ends + [max(0.0, t - now) for t, _ in timers])
        now += step
        for entries in on.values():
            for entry in entries:
                entry[0] -= step / len(entries)
                if entry[0] < 1e-6:
                    active.remove(entry)
                    timers.append((now + LAG, entry[2]))
        if "F" in starts and relayed >= RELAYED:
            timers += [(now, event) for event in starts.pop("F")]
        due = sorted(t for t in timers if t[0] <= now + 1e-6)
        for timer in due:
            timers.remove(timer)
            array, slot, part = timer[1]
            if array == "swap":
                swaps[(slot, part)] -= 1
                if swaps[(slot, part)] == 0:
                    starts[slot] = [(slot, k, p) for k in (OWN_X, OWN) for p in range(PARTS[slot])]
                    if slot == "G":
                        timers += [(now, event) for event in starts.pop("G")]
                        timers += [(now + 0.1, ('A', OWN_X, 0)), (now + 0.2, ('F', START, 0)), (now + 0.3, ('A', OWN, 1)), (now + 0.4, ('A', OWN_X, 1))]
                continue
            order.append((now, array, slot, part))
            send(array, slot, part)
            relayed += array == "G" and slot in (1, 4)
            if slot == START:
                for key in ("x", "+z", "-z"):
                    active.append([1.0 * UNIT, key, ("swap", "F", 0)])
            if slot < OWN:
                continue
            seen[(array, part)] = seen.get((array, part), 0) + 1
            if all(seen.get(("G", p)) == 16 for p in range(PARTS["G"])):
                for p in range(PARTS["A"]):
                    if seen.get(("A", p)) == 8 and ("L", p, 0) not in seen:
                        seen[("L", p, 0)] = 1
                        timers += [(now + 1.5, ("L", OWN, p)), (now + 1.51, ("L", OWN_X, p))]
    return order


def pick(index, values):
    chosen = values[0]
    for position, value in enumerate(values[1:], 1):
        chosen = jnp.where(index == position, value, chosen)
    return chosen


def kernel(order, grad, outer, inner, result, a_buf, g_buf, f_buf, l_buf, l_sum, c_sum, *sems):
    send_sem = dict(zip("AGFL", sems[0:4]))
    recv_sem = dict(zip("AGFL", sems[4:8]))
    swap_send, swap_recv, local_sem, out_sem = sems[8:]
    row, col = lax.axis_index("row"), lax.axis_index("col")
    y, x_lo, core = row // 4, (row // 2) % 2, row % 2
    z, x_hi = col // 2, col % 2

    def row_of(step, other, sibling=0):
        return ((y + step) % 4) * 4 + (x_lo + other) % 2 * 2 + (core + sibling) % 2

    def col_of(step, other):
        return ((z + step) % 4) * 2 + (x_hi + other) % 2

    def device(array, link):
        if link == "core":
            return (row_of(0, 0, 1), col)
        step, other = {"x": (0, 1), "+": (1, 0), "-": (3, 0)}[link]
        return (row, col_of(step, other)) if array in "AL" else (row_of(step, other), col)

    def block_id(array, slot, part):
        step, other, sibling = relative(slot, part)
        return col_of(step, other) if array in "AL" else row_of(step, other, sibling)

    buffers = {"A": a_buf, "G": g_buf, "F": f_buf, "L": l_buf}

    def view(array, block, part):
        buffer = buffers[array]
        if array == "F":
            width = buffer.shape[2] // PARTS["F"]
            return buffer.at[block, :, pl.ds(part * width, width)]
        height = buffer.shape[1] // PARTS[array]
        return buffer.at[block, pl.ds(part * height, height), :]

    def copy(array, slot, part, link, there):
        here = view(array, block_id(array, slot, part), part)
        return pltpu.make_async_remote_copy(
            src_ref=here,
            dst_ref=here,
            send_sem=send_sem[array].at[there, part],
            recv_sem=recv_sem[array].at[there, part],
            device_id=device(array, link),
            device_id_type=MESH,
        )

    def wait_recv(array, slot, part):
        here = view(array, block_id(array, slot, part), part)
        pltpu.make_async_remote_copy(
            src_ref=here,
            dst_ref=here,
            send_sem=send_sem[array].at[slot, part],
            recv_sem=recv_sem[array].at[slot, part],
            device_id=device(array, "x"),
            device_id_type=MESH,
        ).wait_recv()

    sent = []

    def forward(array, slot, part):
        for link, there in plan(array, slot, part):
            outgoing = copy(array, slot, part, link, there)
            outgoing.start()
            sent.append(outgoing)

    locals_ = [
        pltpu.make_async_copy(outer, a_buf.at[col], local_sem.at[0]),
        pltpu.make_async_copy(
            grad.at[:, pl.ds(pl.multiple_of(col * 512, 512), 512)],
            g_buf.at[row, pl.ds(pl.multiple_of(col * 64, 64), 64), :],
            local_sem.at[1],
        ),
        pltpu.make_async_copy(
            inner.at[:, pl.ds(pl.multiple_of(col * 2048, 2048), 2048)],
            f_buf.at[row, pl.ds(pl.multiple_of(col * 32, 32), 32), :],
            local_sem.at[2],
        ),
    ]
    for one in locals_:
        one.start()

    barrier = pltpu.get_barrier_semaphore()
    peers = [(row, lax.rem(col + k, 8)) for k in range(1, 8)]
    peers += [device("G", link) for link in ("x", "+", "-", "core")]
    for peer in peers:
        pl.semaphore_signal(barrier, inc=1, device_id=peer, device_id_type=MESH)
    pl.semaphore_wait(barrier, len(peers))

    def swap(which, k):
        source, buffer, height, width = ((grad, g_buf, 64, 512), (inner, f_buf, 32, 2048))[which]
        to = lax.rem(col + k, 8)
        return pltpu.make_async_remote_copy(
            src_ref=source.at[:, pl.ds(pl.multiple_of(to * width, width), width)],
            dst_ref=buffer.at[row, pl.ds(pl.multiple_of(col * height, height), height), :],
            send_sem=swap_send.at[which, k],
            recv_sem=swap_recv.at[which, k],
            device_id=(row, to),
            device_id_type=MESH,
        )

    def swap_wait(which, k):
        source, buffer, height, width = ((grad, g_buf, 64, 512), (inner, f_buf, 32, 2048))[which]
        sender = lax.rem(col + 8 - k, 8)
        pltpu.make_async_remote_copy(
            src_ref=source.at[:, pl.ds(0, width)],
            dst_ref=buffer.at[row, pl.ds(pl.multiple_of(sender * height, height), height), :],
            send_sem=swap_send.at[which, k],
            recv_sem=swap_recv.at[which, k],
            device_id=(row, sender),
            device_id_type=MESH,
        ).wait_recv()

    def start_swap(which):
        for k in (4, 3, 5, 2, 6, 1, 7):
            outgoing = swap(which, k)
            outgoing.start()
            sent.append(outgoing)

    start_swap(0)

    def add_left(block, part):
        rows = pl.ds(part * 256 if isinstance(part, int) else pl.multiple_of(part * 256, 256), 256)
        grads = g_buf[pl.ds(block * 2, 2)].reshape(1024, 512)
        l_sum[rows, :] += jnp.dot(a_buf[block, rows, :], grads, preferred_element_type=jnp.float32)

    def add_result(block, part):
        columns = pl.ds(part * 512 if isinstance(part, int) else pl.multiple_of(part * 512, 512), 512)
        weights = f_buf[pl.ds(block * 2, 2), :, columns].reshape(512, 512)
        c_sum[:, columns] += jnp.dot(l_buf[block], weights, preferred_element_type=jnp.float32)

    def each(pairs, act):
        if len(pairs) < 2:
            for pair in pairs:
                act(*pair)
            return

        @pl.loop(0, len(pairs))
        def _(k):
            act(pick(k, [p[0] for p in pairs]), pick(k, [p[1] for p in pairs]))

    counts = dict.fromkeys("AGFL", 0)
    counts.update({("F", p): 0 for p in range(PARTS["F"])})
    begun = set()
    pending_left, ready_l, ready_f, out_copies = [], [], [], []
    blocks_l = {}
    done = [0] * PARTS["F"]

    def multiply(pairs):
        last = any(done[p] == 7 for _, p in pairs)
        for group in [[pair] for pair in pairs] if last else [pairs]:
            each(group, add_result)
            for _, p in group:
                done[p] += 1
                if done[p] == 8:
                    columns = pl.ds(p * 512, 512)
                    out = pltpu.make_async_copy(c_sum.at[:, columns], result.at[:, columns], out_sem.at[p])
                    out.start()
                    out_copies.append(out)

    for _, array, slot, part in order:
        if slot == START:
            start_swap(1)
            l_sum[...] = jnp.zeros_like(l_sum)

            @pl.loop(0, 8)
            def _(k):
                rows = pl.ds(pl.multiple_of(k * 64, 64), 64)
                c_sum[rows, :] = jnp.zeros((64, 2048), jnp.float32)

            continue
        if array in "GF" and array not in begun:
            begun.add(array)
            which = "GF".index(array)
            locals_[1 + which].wait()
            for k in range(1, 8):
                swap_wait(which, k)
        if array == "A" and array not in begun:
            begun.add(array)
            locals_[0].wait()
        if array == "L" and slot == OWN:
            l_buf[col, pl.ds(part * 256, 256), :] = l_sum[pl.ds(part * 256, 256), :].astype(jnp.bfloat16)
        if slot >= 0:
            wait_recv(array, slot, part)
        if slot < 7:
            forward(array, slot, part)
        if slot < OWN:
            continue
        counts[array] += 1
        if array == "A":
            pending_left.append((block_id("A", slot, part), part))
        if array in "AG" and counts["G"] == 16 * PARTS["G"]:
            each(pending_left, add_left)
            pending_left.clear()
        if array == "L":
            place = relative(slot, part)
            blocks_l[place] = blocks_l.get(place, 0) + 1
            if blocks_l[place] == PARTS["L"]:
                ready_l.append(block_id("L", slot, part))
                multiply([(ready_l[-1], p) for p in ready_f])
        if array == "F":
            counts[("F", part)] += 1
            if counts[("F", part)] == 16:
                ready_f.append(part)
                multiply([(block, part) for block in ready_l])

    for one in sent:
        one.wait_send()
    for out in out_copies:
        out.wait()


def per_device(grad_flat, out_factor_inv, in_factor_inv):
    order = schedule()
    dma = pltpu.SemaphoreType.DMA
    return pl.pallas_call(
        functools.partial(kernel, order),
        out_shape=jax.ShapeDtypeStruct((512, 2048), jnp.float32),
        in_specs=[pl.BlockSpec(memory_space=pl.ANY)] * 3,
        out_specs=pl.BlockSpec(memory_space=pl.ANY),
        scratch_shapes=[
            pltpu.VMEM((8, 512, 1024), jnp.bfloat16),
            pltpu.VMEM((16, 512, 512), jnp.bfloat16),
            pltpu.VMEM((16, 256, 2048), jnp.bfloat16),
            pltpu.VMEM((8, 512, 512), jnp.bfloat16),
            pltpu.VMEM((512, 512), jnp.float32),
            pltpu.VMEM((512, 2048), jnp.float32),
            dma((7, PARTS["A"])),
            dma((15, PARTS["G"])),
            dma((15, PARTS["F"])),
            dma((7, PARTS["L"])),
            dma((7, PARTS["A"])),
            dma((15, PARTS["G"])),
            dma((15, PARTS["F"])),
            dma((7, PARTS["L"])),
            dma((2, 8)),
            dma((2, 8)),
            dma((3,)),
            dma((PARTS["F"],)),
        ],
        compiler_params=pltpu.CompilerParams(
            collective_id=0, has_side_effects=True, vmem_limit_bytes=60 * 2**20
        ),
    )(grad_flat, out_factor_inv, in_factor_inv)


def solution(mesh):
    return jax.shard_map(
        per_device,
        mesh=mesh,
        in_specs=(P(("row", "col"), None), P("row", "col"), P(("row", "col"), None)),
        out_specs=P("row", "col"),
        check_vma=False,
    )
```

```python
import functools

import jax
import jax.numpy as jnp
from jax import lax
from jax.experimental import pallas as pl
from jax.experimental.pallas import tpu as pltpu
from jax.sharding import PartitionSpec as P

MESH = pl.DeviceIdType.MESH

PARTS = {"A": 2, "L": 2, "G": 2, "F": 4}
UNITS = {"A": 1.0, "L": 0.5, "G": 0.5, "F": 0.5}
RELIEF = {"A": False, "L": True, "G": False, "F": False}
OWN, OWN_X, START = -1, -2, -3
RELAYED = 4
STEP = 2
UNIT, LAG, FIFO = 12.0, 3.0, True


def plan(array, slot, part):
    ahead, behind = ("+", "-") if part % 2 == 0 else ("-", "+")
    sends = {
        OWN: [(ahead, 1), (behind, 2)],
        OWN_X: [("x", 0)],
        0: [(ahead, 3)] + ([] if RELIEF[array] or (array == "A" and part == 0) else [(behind, 4)]),
        1: [(ahead, 5)],
        2: [("x", 4)] if RELIEF[array] or (array == "A" and part == 0) else [],
        4: [(behind, 6)],
    }.get(slot, [])
    if array in "GF" and OWN <= slot < 7:
        sends = sends + [("core", 8 + slot)]
    return sends


def relative(slot, part):
    sibling, slot = (1, slot - 8) if slot >= 7 else (0, slot)
    step, other = {OWN: (0, 0), OWN_X: (0, 0), 0: (0, 1), 1: (3, 0), 2: (1, 0), 3: (3, 1), 4: (1, 1), 5: (2, 0), 6: (2, 1)}[slot]
    return (step if part % 2 == 0 else (4 - step) % 4), other, sibling


def schedule():
    now, active, timers, order, seen = 0.0, [], [], [], {}
    swaps, starts, relayed = {("G", 0): 3, ("F", 0): 3}, {}, 0

    def send(array, slot, part):
        for link, there in plan(array, slot, part):
            key = link if link in ("x", "core") else link + ("z" if array in "AL" else "y")
            active.append([UNITS[array] * (UNIT if link != "core" else 1.8), key, (array, there, part)])

    for key in ("x", "+z", "-z"):
        active.append([0.5 * UNIT, key, ("swap", "G", 0)])
    timers += [(0.5, ("A", OWN, 0))]
    while active or timers:
        on = {}
        for entry in active:
            on.setdefault(entry[1], []).append(entry)
        if FIFO:
            on = {key: entries[:1] for key, entries in on.items()}
        ends = [entry[0] * len(entries) for entries in on.values() for entry in entries]
        step = min(ends + [max(0.0, t - now) for t, _ in timers])
        now += step
        for entries in on.values():
            for entry in entries:
                entry[0] -= step / len(entries)
                if entry[0] < 1e-6:
                    active.remove(entry)
                    timers.append((now + LAG, entry[2]))
        if "F" in starts and relayed >= RELAYED:
            timers += [(now, event) for event in starts.pop("F")]
        due = sorted(t for t in timers if t[0] <= now + 1e-6)
        for timer in due:
            timers.remove(timer)
            array, slot, part = timer[1]
            if array == "swap":
                swaps[(slot, part)] -= 1
                if swaps[(slot, part)] == 0:
                    starts[slot] = [(slot, k, p) for k in (OWN_X, OWN) for p in range(PARTS[slot])]
                    if slot == "G":
                        timers += [(now, event) for event in starts.pop("G")]
                        timers += [(now + 0.1, ('A', OWN_X, 0)), (now + 0.2, ('F', START, 0)), (now + 0.3, ('A', OWN, 1)), (now + 0.4, ('A', OWN_X, 1))]
                continue
            order.append((now, array, slot, part))
            send(array, slot, part)
            relayed += array == "G" and slot in (1, 4)
            if slot == START:
                for key in ("x", "+z", "-z"):
                    active.append([1.0 * UNIT, key, ("swap", "F", 0)])
            if slot < OWN:
                continue
            seen[(array, part)] = seen.get((array, part), 0) + 1
            if all(seen.get(("G", p)) == 16 for p in range(PARTS["G"])):
                for p in range(PARTS["A"]):
                    if seen.get(("A", p)) == 8 and ("L", p, 0) not in seen:
                        seen[("L", p, 0)] = 1
                        timers += [(now + 1.5, ("L", OWN, p)), (now + 1.51, ("L", OWN_X, p))]
    return order


def pick(index, values):
    chosen = values[0]
    for position, value in enumerate(values[1:], 1):
        chosen = jnp.where(index == position, value, chosen)
    return chosen


def kernel(order, grad, outer, inner, result, a_buf, g_buf, f_buf, l_buf, l_sum, c_sum, *sems):
    send_sem = dict(zip("AGFL", sems[0:4]))
    recv_sem = dict(zip("AGFL", sems[4:8]))
    swap_send, swap_recv, local_sem, out_sem = sems[8:]
    row, col = lax.axis_index("row"), lax.axis_index("col")
    y, x_lo, core = row // 4, (row // 2) % 2, row % 2
    z, x_hi = col // 2, col % 2

    def row_of(step, other, sibling=0):
        return ((y + step) % 4) * 4 + (x_lo + other) % 2 * 2 + (core + sibling) % 2

    def col_of(step, other):
        return ((z + step) % 4) * 2 + (x_hi + other) % 2

    def device(array, link):
        if link == "core":
            return (row_of(0, 0, 1), col)
        step, other = {"x": (0, 1), "+": (1, 0), "-": (3, 0)}[link]
        return (row, col_of(step, other)) if array in "AL" else (row_of(step, other), col)

    def block_id(array, slot, part):
        step, other, sibling = relative(slot, part)
        return col_of(step, other) if array in "AL" else row_of(step, other, sibling)

    buffers = {"A": a_buf, "G": g_buf, "F": f_buf, "L": l_buf}

    def view(array, block, part):
        buffer = buffers[array]
        if array == "F":
            width = buffer.shape[2] // PARTS["F"]
            return buffer.at[block, :, pl.ds(part * width, width)]
        height = buffer.shape[1] // PARTS[array]
        return buffer.at[block, pl.ds(part * height, height), :]

    def copy(array, slot, part, link, there):
        here = view(array, block_id(array, slot, part), part)
        return pltpu.make_async_remote_copy(
            src_ref=here,
            dst_ref=here,
            send_sem=send_sem[array].at[there, part],
            recv_sem=recv_sem[array].at[there, part],
            device_id=device(array, link),
            device_id_type=MESH,
        )

    def wait_recv(array, slot, part):
        here = view(array, block_id(array, slot, part), part)
        pltpu.make_async_remote_copy(
            src_ref=here,
            dst_ref=here,
            send_sem=send_sem[array].at[slot, part],
            recv_sem=recv_sem[array].at[slot, part],
            device_id=device(array, "x"),
            device_id_type=MESH,
        ).wait_recv()

    sent = []

    def forward(array, slot, part):
        for link, there in plan(array, slot, part):
            outgoing = copy(array, slot, part, link, there)
            outgoing.start()
            sent.append(outgoing)

    locals_ = [
        pltpu.make_async_copy(outer, a_buf.at[col], local_sem.at[0]),
        pltpu.make_async_copy(
            grad.at[:, pl.ds(pl.multiple_of(col * 512, 512), 512)],
            g_buf.at[row, pl.ds(pl.multiple_of(col * 64, 64), 64), :],
            local_sem.at[1],
        ),
        pltpu.make_async_copy(
            inner.at[:, pl.ds(pl.multiple_of(col * 2048, 2048), 2048)],
            f_buf.at[row, pl.ds(pl.multiple_of(col * 32, 32), 32), :],
            local_sem.at[2],
        ),
    ]
    for one in locals_:
        one.start()

    barrier = pltpu.get_barrier_semaphore()
    peers = [(row, lax.rem(col + k, 8)) for k in range(1, 8)]
    peers += [device("G", link) for link in ("x", "+", "-", "core")]
    for peer in peers:
        pl.semaphore_signal(barrier, inc=1, device_id=peer, device_id_type=MESH)
    pl.semaphore_wait(barrier, len(peers))

    def swap(which, k):
        source, buffer, height, width = ((grad, g_buf, 64, 512), (inner, f_buf, 32, 2048))[which]
        to = lax.rem(col + k, 8)
        return pltpu.make_async_remote_copy(
            src_ref=source.at[:, pl.ds(pl.multiple_of(to * width, width), width)],
            dst_ref=buffer.at[row, pl.ds(pl.multiple_of(col * height, height), height), :],
            send_sem=swap_send.at[which, k],
            recv_sem=swap_recv.at[which, k],
            device_id=(row, to),
            device_id_type=MESH,
        )

    def swap_wait(which, k):
        source, buffer, height, width = ((grad, g_buf, 64, 512), (inner, f_buf, 32, 2048))[which]
        sender = lax.rem(col + 8 - k, 8)
        pltpu.make_async_remote_copy(
            src_ref=source.at[:, pl.ds(0, width)],
            dst_ref=buffer.at[row, pl.ds(pl.multiple_of(sender * height, height), height), :],
            send_sem=swap_send.at[which, k],
            recv_sem=swap_recv.at[which, k],
            device_id=(row, sender),
            device_id_type=MESH,
        ).wait_recv()

    def start_swap(which):
        for k in (4, 3, 5, 2, 6, 1, 7):
            outgoing = swap(which, k)
            outgoing.start()
            sent.append(outgoing)

    start_swap(0)

    def add_left(block, part):
        rows = pl.ds(part * 256 if isinstance(part, int) else pl.multiple_of(part * 256, 256), 256)
        grads = g_buf[pl.ds(block * 2, 2)].reshape(1024, 512)
        l_sum[rows, :] += jnp.dot(a_buf[block, rows, :], grads, preferred_element_type=jnp.float32)

    def add_result(block, part):
        columns = pl.ds(part * 512 if isinstance(part, int) else pl.multiple_of(part * 512, 512), 512)
        weights = f_buf[pl.ds(block * 2, 2), :, columns].reshape(512, 512)
        c_sum[:, columns] += jnp.dot(l_buf[block], weights, preferred_element_type=jnp.float32)

    def each(pairs, act):
        if len(pairs) < 2:
            for pair in pairs:
                act(*pair)
            return

        @pl.loop(0, len(pairs))
        def _(k):
            act(pick(k, [p[0] for p in pairs]), pick(k, [p[1] for p in pairs]))

    counts = dict.fromkeys("AGFL", 0)
    counts.update({("F", p): 0 for p in range(PARTS["F"])})
    begun, pending_c = set(), []
    pending_left, ready_l, ready_f, out_copies = [], [], [], []
    blocks_l = {}
    done = [0] * PARTS["F"]

    def multiply(pairs):
        last = any(done[p] == 7 for _, p in pairs)
        for group in [[pair] for pair in pairs] if last else [pairs]:
            each(group, add_result)
            for _, p in group:
                done[p] += 1
                if done[p] == 8:
                    columns = pl.ds(p * 512, 512)
                    out = pltpu.make_async_copy(c_sum.at[:, columns], result.at[:, columns], out_sem.at[p])
                    out.start()
                    out_copies.append(out)

    for _, array, slot, part in order:
        if slot == START:
            start_swap(1)
            l_sum[...] = jnp.zeros_like(l_sum)

            @pl.loop(0, 8)
            def _(k):
                rows = pl.ds(pl.multiple_of(k * 64, 64), 64)
                c_sum[rows, :] = jnp.zeros((64, 2048), jnp.float32)

            continue
        if array in "GF" and array not in begun:
            begun.add(array)
            which = "GF".index(array)
            locals_[1 + which].wait()
            for k in range(1, 8):
                swap_wait(which, k)
        if array == "A" and array not in begun:
            begun.add(array)
            locals_[0].wait()
        if array == "L" and slot == OWN:
            each([u for u in pending_left if u[1] == part], add_left)
            pending_left[:] = [u for u in pending_left if u[1] != part]
            l_buf[col, pl.ds(part * 256, 256), :] = l_sum[pl.ds(part * 256, 256), :].astype(jnp.bfloat16)
        if slot >= 0:
            wait_recv(array, slot, part)
        if slot < 7:
            forward(array, slot, part)
        if slot < OWN:
            continue
        counts[array] += 1
        if array == "A":
            pending_left.append((block_id("A", slot, part), part))
        if array in "AG" and counts["G"] == 16 * PARTS["G"]:
            pass
        if array == "L":
            place = relative(slot, part)
            blocks_l[place] = blocks_l.get(place, 0) + 1
            if blocks_l[place] == PARTS["L"]:
                ready_l.append(block_id("L", slot, part))
                pending_c += [(ready_l[-1], p) for p in ready_f]
        if array == "F":
            counts[("F", part)] += 1
            if counts[("F", part)] == 16:
                ready_f.append(part)
                pending_c += [(block, part) for block in ready_l]
        if counts["G"] == 16 * PARTS["G"] and pending_left:
            each(pending_left[:STEP], add_left)
            del pending_left[:STEP]
        elif pending_c:
            multiply(pending_c[:STEP])
            del pending_c[:STEP]
    multiply(pending_c)

    for one in sent:
        one.wait_send()
    for out in out_copies:
        out.wait()


def per_device(grad_flat, out_factor_inv, in_factor_inv):
    order = schedule()
    dma = pltpu.SemaphoreType.DMA
    return pl.pallas_call(
        functools.partial(kernel, order),
        out_shape=jax.ShapeDtypeStruct((512, 2048), jnp.float32),
        in_specs=[pl.BlockSpec(memory_space=pl.ANY)] * 3,
        out_specs=pl.BlockSpec(memory_space=pl.ANY),
        scratch_shapes=[
            pltpu.VMEM((8, 512, 1024), jnp.bfloat16),
            pltpu.VMEM((16, 512, 512), jnp.bfloat16),
            pltpu.VMEM((16, 256, 2048), jnp.bfloat16),
            pltpu.VMEM((8, 512, 512), jnp.bfloat16),
            pltpu.VMEM((512, 512), jnp.float32),
            pltpu.VMEM((512, 2048), jnp.float32),
            dma((7, PARTS["A"])),
            dma((15, PARTS["G"])),
            dma((15, PARTS["F"])),
            dma((7, PARTS["L"])),
            dma((7, PARTS["A"])),
            dma((15, PARTS["G"])),
            dma((15, PARTS["F"])),
            dma((7, PARTS["L"])),
            dma((2, 8)),
            dma((2, 8)),
            dma((3,)),
            dma((PARTS["F"],)),
        ],
        compiler_params=pltpu.CompilerParams(
            collective_id=0, has_side_effects=True, vmem_limit_bytes=60 * 2**20
        ),
    )(grad_flat, out_factor_inv, in_factor_inv)


def solution(mesh):
    return jax.shard_map(
        per_device,
        mesh=mesh,
        in_specs=(P(("row", "col"), None), P("row", "col"), P(("row", "col"), None)),
        out_specs=P("row", "col"),
        check_vma=False,
    )
```

```python
import functools

import jax
import jax.numpy as jnp
from jax import lax
from jax.experimental import pallas as pl
from jax.experimental.pallas import tpu as pltpu
from jax.sharding import PartitionSpec as P

MESH = pl.DeviceIdType.MESH

PARTS = {"A": 2, "L": 2, "G": 2, "F": 4}
UNITS = {"A": 1.0, "L": 0.5, "G": 0.5, "F": 0.5}
RELIEF = {"A": False, "L": True, "G": False, "F": False}
OWN, OWN_X, START = -1, -2, -3
RELAYED = 4
STEP = 2
UNIT, LAG, FIFO = 12.0, 3.0, True


def plan(array, slot, part):
    ahead, behind = ("+", "-") if part % 2 == 0 else ("-", "+")
    sends = {
        OWN: [(ahead, 1), (behind, 2)],
        OWN_X: [("x", 0)],
        0: [(ahead, 3)] + ([] if RELIEF[array] or (array == "A" and part == 1) else [(behind, 4)]),
        1: [(ahead, 5)],
        2: [("x", 4)] if RELIEF[array] or (array == "A" and part == 1) else [],
        4: [(behind, 6)],
    }.get(slot, [])
    if array in "GF" and OWN <= slot < 7:
        sends = sends + [("core", 8 + slot)]
    return sends


def relative(slot, part):
    sibling, slot = (1, slot - 8) if slot >= 7 else (0, slot)
    step, other = {OWN: (0, 0), OWN_X: (0, 0), 0: (0, 1), 1: (3, 0), 2: (1, 0), 3: (3, 1), 4: (1, 1), 5: (2, 0), 6: (2, 1)}[slot]
    return (step if part % 2 == 0 else (4 - step) % 4), other, sibling


def schedule():
    now, active, timers, order, seen = 0.0, [], [], [], {}
    swaps, starts, relayed = {("G", 0): 3, ("F", 0): 3}, {}, 0

    def send(array, slot, part):
        for link, there in plan(array, slot, part):
            key = link if link in ("x", "core") else link + ("z" if array in "AL" else "y")
            active.append([UNITS[array] * (UNIT if link != "core" else 1.8), key, (array, there, part)])

    for key in ("x", "+z", "-z"):
        active.append([0.5 * UNIT, key, ("swap", "G", 0)])
    timers += [(0.5, ("A", OWN, 0))]
    while active or timers:
        on = {}
        for entry in active:
            on.setdefault(entry[1], []).append(entry)
        if FIFO:
            on = {key: entries[:1] for key, entries in on.items()}
        ends = [entry[0] * len(entries) for entries in on.values() for entry in entries]
        step = min(ends + [max(0.0, t - now) for t, _ in timers])
        now += step
        for entries in on.values():
            for entry in entries:
                entry[0] -= step / len(entries)
                if entry[0] < 1e-6:
                    active.remove(entry)
                    timers.append((now + LAG, entry[2]))
        if "F" in starts and relayed >= RELAYED:
            timers += [(now, event) for event in starts.pop("F")]
        due = sorted(t for t in timers if t[0] <= now + 1e-6)
        for timer in due:
            timers.remove(timer)
            array, slot, part = timer[1]
            if array == "swap":
                swaps[(slot, part)] -= 1
                if swaps[(slot, part)] == 0:
                    starts[slot] = [(slot, k, p) for k in (OWN_X, OWN) for p in range(PARTS[slot])]
                    if slot == "G":
                        timers += [(now, event) for event in starts.pop("G")]
                        timers += [(now + 0.1, ('A', OWN_X, 0)), (now + 0.2, ('F', START, 0)), (now + 0.3, ('A', OWN, 1)), (now + 0.4, ('A', OWN_X, 1))]
                continue
            order.append((now, array, slot, part))
            send(array, slot, part)
            relayed += array == "G" and slot in (1, 4)
            if slot == START:
                for key in ("x", "+z", "-z"):
                    active.append([1.0 * UNIT, key, ("swap", "F", 0)])
            if slot < OWN:
                continue
            seen[(array, part)] = seen.get((array, part), 0) + 1
            if all(seen.get(("G", p)) == 16 for p in range(PARTS["G"])):
                for p in range(PARTS["A"]):
                    if seen.get(("A", p)) == 8 and ("L", p, 0) not in seen:
                        seen[("L", p, 0)] = 1
                        timers += [(now + 1.5, ("L", OWN, p)), (now + 1.51, ("L", OWN_X, p))]
    return order


def pick(index, values):
    chosen = values[0]
    for position, value in enumerate(values[1:], 1):
        chosen = jnp.where(index == position, value, chosen)
    return chosen


def kernel(order, grad, outer, inner, result, a_buf, g_buf, f_buf, l_buf, l_sum, c_sum, *sems):
    send_sem = dict(zip("AGFL", sems[0:4]))
    recv_sem = dict(zip("AGFL", sems[4:8]))
    swap_send, swap_recv, local_sem, out_sem = sems[8:]
    row, col = lax.axis_index("row"), lax.axis_index("col")
    y, x_lo, core = row // 4, (row // 2) % 2, row % 2
    z, x_hi = col // 2, col % 2

    def row_of(step, other, sibling=0):
        return ((y + step) % 4) * 4 + (x_lo + other) % 2 * 2 + (core + sibling) % 2

    def col_of(step, other):
        return ((z + step) % 4) * 2 + (x_hi + other) % 2

    def device(array, link):
        if link == "core":
            return (row_of(0, 0, 1), col)
        step, other = {"x": (0, 1), "+": (1, 0), "-": (3, 0)}[link]
        return (row, col_of(step, other)) if array in "AL" else (row_of(step, other), col)

    def block_id(array, slot, part):
        step, other, sibling = relative(slot, part)
        return col_of(step, other) if array in "AL" else row_of(step, other, sibling)

    buffers = {"A": a_buf, "G": g_buf, "F": f_buf, "L": l_buf}

    def view(array, block, part):
        buffer = buffers[array]
        if array == "F":
            width = buffer.shape[2] // PARTS["F"]
            return buffer.at[block, :, pl.ds(part * width, width)]
        height = buffer.shape[1] // PARTS[array]
        return buffer.at[block, pl.ds(part * height, height), :]

    def copy(array, slot, part, link, there):
        here = view(array, block_id(array, slot, part), part)
        return pltpu.make_async_remote_copy(
            src_ref=here,
            dst_ref=here,
            send_sem=send_sem[array].at[there, part],
            recv_sem=recv_sem[array].at[there, part],
            device_id=device(array, link),
            device_id_type=MESH,
        )

    def wait_recv(array, slot, part):
        here = view(array, block_id(array, slot, part), part)
        pltpu.make_async_remote_copy(
            src_ref=here,
            dst_ref=here,
            send_sem=send_sem[array].at[slot, part],
            recv_sem=recv_sem[array].at[slot, part],
            device_id=device(array, "x"),
            device_id_type=MESH,
        ).wait_recv()

    sent = []

    def forward(array, slot, part):
        for link, there in plan(array, slot, part):
            outgoing = copy(array, slot, part, link, there)
            outgoing.start()
            sent.append(outgoing)

    locals_ = [
        pltpu.make_async_copy(outer, a_buf.at[col], local_sem.at[0]),
        pltpu.make_async_copy(
            grad.at[:, pl.ds(pl.multiple_of(col * 512, 512), 512)],
            g_buf.at[row, pl.ds(pl.multiple_of(col * 64, 64), 64), :],
            local_sem.at[1],
        ),
        pltpu.make_async_copy(
            inner.at[:, pl.ds(pl.multiple_of(col * 2048, 2048), 2048)],
            f_buf.at[row, pl.ds(pl.multiple_of(col * 32, 32), 32), :],
            local_sem.at[2],
        ),
    ]
    for one in locals_:
        one.start()

    barrier = pltpu.get_barrier_semaphore()
    peers = [(row, lax.rem(col + k, 8)) for k in range(1, 8)]
    peers += [device("G", link) for link in ("x", "+", "-", "core")]
    for peer in peers:
        pl.semaphore_signal(barrier, inc=1, device_id=peer, device_id_type=MESH)
    pl.semaphore_wait(barrier, len(peers))

    def swap(which, k):
        source, buffer, height, width = ((grad, g_buf, 64, 512), (inner, f_buf, 32, 2048))[which]
        to = lax.rem(col + k, 8)
        return pltpu.make_async_remote_copy(
            src_ref=source.at[:, pl.ds(pl.multiple_of(to * width, width), width)],
            dst_ref=buffer.at[row, pl.ds(pl.multiple_of(col * height, height), height), :],
            send_sem=swap_send.at[which, k],
            recv_sem=swap_recv.at[which, k],
            device_id=(row, to),
            device_id_type=MESH,
        )

    def swap_wait(which, k):
        source, buffer, height, width = ((grad, g_buf, 64, 512), (inner, f_buf, 32, 2048))[which]
        sender = lax.rem(col + 8 - k, 8)
        pltpu.make_async_remote_copy(
            src_ref=source.at[:, pl.ds(0, width)],
            dst_ref=buffer.at[row, pl.ds(pl.multiple_of(sender * height, height), height), :],
            send_sem=swap_send.at[which, k],
            recv_sem=swap_recv.at[which, k],
            device_id=(row, sender),
            device_id_type=MESH,
        ).wait_recv()

    def start_swap(which):
        for k in (4, 3, 5, 2, 6, 1, 7):
            outgoing = swap(which, k)
            outgoing.start()
            sent.append(outgoing)

    start_swap(0)

    def add_left(block, part):
        rows = pl.ds(part * 256 if isinstance(part, int) else pl.multiple_of(part * 256, 256), 256)
        grads = g_buf[pl.ds(block * 2, 2)].reshape(1024, 512)
        l_sum[rows, :] += jnp.dot(a_buf[block, rows, :], grads, preferred_element_type=jnp.float32)

    def add_result(block, part):
        columns = pl.ds(part * 512 if isinstance(part, int) else pl.multiple_of(part * 512, 512), 512)
        weights = f_buf[pl.ds(block * 2, 2), :, columns].reshape(512, 512)
        c_sum[:, columns] += jnp.dot(l_buf[block], weights, preferred_element_type=jnp.float32)

    def each(pairs, act):
        if len(pairs) < 2:
            for pair in pairs:
                act(*pair)
            return

        @pl.loop(0, len(pairs))
        def _(k):
            act(pick(k, [p[0] for p in pairs]), pick(k, [p[1] for p in pairs]))

    counts = dict.fromkeys("AGFL", 0)
    counts.update({("F", p): 0 for p in range(PARTS["F"])})
    begun, pending_c = set(), []
    pending_left, ready_l, ready_f, out_copies = [], [], [], []
    blocks_l = {}
    done = [0] * PARTS["F"]

    def multiply(pairs):
        last = any(done[p] == 7 for _, p in pairs)
        for group in [[pair] for pair in pairs] if last else [pairs]:
            each(group, add_result)
            for _, p in group:
                done[p] += 1
                if done[p] == 8:
                    columns = pl.ds(p * 512, 512)
                    out = pltpu.make_async_copy(c_sum.at[:, columns], result.at[:, columns], out_sem.at[p])
                    out.start()
                    out_copies.append(out)

    for _, array, slot, part in order:
        if slot == START:
            start_swap(1)
            l_sum[...] = jnp.zeros_like(l_sum)

            @pl.loop(0, 8)
            def _(k):
                rows = pl.ds(pl.multiple_of(k * 64, 64), 64)
                c_sum[rows, :] = jnp.zeros((64, 2048), jnp.float32)

            continue
        if array in "GF" and array not in begun:
            begun.add(array)
            which = "GF".index(array)
            locals_[1 + which].wait()
            for k in range(1, 8):
                swap_wait(which, k)
        if array == "A" and array not in begun:
            begun.add(array)
            locals_[0].wait()
        if array == "L" and slot == OWN:
            each([u for u in pending_left if u[1] == part], add_left)
            pending_left[:] = [u for u in pending_left if u[1] != part]
            l_buf[col, pl.ds(part * 256, 256), :] = l_sum[pl.ds(part * 256, 256), :].astype(jnp.bfloat16)
        if slot >= 0:
            wait_recv(array, slot, part)
        if slot < 7:
            forward(array, slot, part)
        if slot < OWN:
            continue
        counts[array] += 1
        if array == "A":
            pending_left.append((block_id("A", slot, part), part))
        if array in "AG" and counts["G"] == 16 * PARTS["G"]:
            pass
        if array == "L":
            place = relative(slot, part)
            blocks_l[place] = blocks_l.get(place, 0) + 1
            if blocks_l[place] == PARTS["L"]:
                ready_l.append(block_id("L", slot, part))
                pending_c += [(ready_l[-1], p) for p in ready_f]
        if array == "F":
            counts[("F", part)] += 1
            if counts[("F", part)] == 16:
                ready_f.append(part)
                pending_c += [(block, part) for block in ready_l]
        if counts["G"] == 16 * PARTS["G"] and pending_left:
            each(pending_left[:STEP], add_left)
            del pending_left[:STEP]
        elif pending_c:
            multiply(pending_c[:STEP])
            del pending_c[:STEP]
    multiply(pending_c)

    for one in sent:
        one.wait_send()
    for out in out_copies:
        out.wait()


def per_device(grad_flat, out_factor_inv, in_factor_inv):
    order = schedule()
    dma = pltpu.SemaphoreType.DMA
    return pl.pallas_call(
        functools.partial(kernel, order),
        out_shape=jax.ShapeDtypeStruct((512, 2048), jnp.float32),
        in_specs=[pl.BlockSpec(memory_space=pl.ANY)] * 3,
        out_specs=pl.BlockSpec(memory_space=pl.ANY),
        scratch_shapes=[
            pltpu.VMEM((8, 512, 1024), jnp.bfloat16),
            pltpu.VMEM((16, 512, 512), jnp.bfloat16),
            pltpu.VMEM((16, 256, 2048), jnp.bfloat16),
            pltpu.VMEM((8, 512, 512), jnp.bfloat16),
            pltpu.VMEM((512, 512), jnp.float32),
            pltpu.VMEM((512, 2048), jnp.float32),
            dma((7, PARTS["A"])),
            dma((15, PARTS["G"])),
            dma((15, PARTS["F"])),
            dma((7, PARTS["L"])),
            dma((7, PARTS["A"])),
            dma((15, PARTS["G"])),
            dma((15, PARTS["F"])),
            dma((7, PARTS["L"])),
            dma((2, 8)),
            dma((2, 8)),
            dma((3,)),
            dma((PARTS["F"],)),
        ],
        compiler_params=pltpu.CompilerParams(
            collective_id=0, has_side_effects=True, vmem_limit_bytes=60 * 2**20
        ),
    )(grad_flat, out_factor_inv, in_factor_inv)


def solution(mesh):
    return jax.shard_map(
        per_device,
        mesh=mesh,
        in_specs=(P(("row", "col"), None), P("row", "col"), P(("row", "col"), None)),
        out_specs=P("row", "col"),
        check_vma=False,
    )
```
